32 devices in a mesh: groups: 2 (over x), gx: 16 (over z, y, core).
Axes of the slice: x: 2, y: 2, z: 4, core: 2. Of those that a mesh axis runs over, the one named last changes fastest.
Arguments:
- tokens: bfloat16 [1024, 16384], P('groups', 'gx'), parts along dimension 0, may hold values from -6 to 6
- token_scale: float32 [1024, 128], P('groups', 'gx'), parts along dimension 0, may hold values from 0.25 to 4
- gate_tiles: bfloat16 [16, 8192, 832], P('gx'), may hold values from -0.046875 to 0.046875
- up_tiles: bfloat16 [16, 8192, 832], P('gx'), may hold values from -0.046875 to 0.046875
- gate_scale: float32 [128, 52], replicated, may hold values from 0.25 to 4
- up_scale: float32 [128, 52], replicated, may hold values from 0.25 to 4
- down_tiles: bfloat16 [16, 832, 8192], P('gx'), may hold values from -0.078125 to 0.078125
- down_scale: float32 [52, 128], replicated, may hold values from 0.25 to 4
Outputs:
- mixed: bfloat16 [1024, 16384], P('groups', 'gx'), parts along dimension 0
The draws below stay inside these ranges and needn't reach their ends.
There are 2 independent parts, one for each index of `groups`. The reference program is written for one: setup_inputs(seed, part) draws one part's arguments, and reference() takes and returns one part's arrays. A program takes and returns all parts, laid end to end along the dimension named above; an argument that names none is the same for every part. Nothing has to cross between parts.
All inputs are finite; a program needn't handle non-finite values.
Results may differ from the reference program's by a relative error of at most 0.0081.
Values may be sent and summed in bfloat16 or wider, within the bound.
A program may use at most 256 MiB of HBM per device.

```python
import math
import jax
import jax.numpy as jnp

D = 16384
FF_SH = 6656
BLK = 128
RO = 8
TOK = 512
RI = 2
N_GX = 16


def steps_of(own_key, dims, cuts, smallest, high):
    def one(position, shards_of):
        heights = jax.random.uniform(jax.random.fold_in(jax.random.fold_in(own_key, 6), position), (shards_of,), jnp.float32, smallest / len(cuts), high / len(cuts))
        return jnp.repeat(jnp.exp(heights), dims[position] // shards_of).reshape((-1,) + (1,) * (len(dims) - position - 1))

    loudness = one(*cuts[0])
    for cut in cuts[1:]:
        loudness = loudness * one(*cut)
    return loudness


def centred(rng, dims, scale, reach, pieces=(), kind=jnp.bfloat16):
    factor_of = steps_of(rng, dims, pieces, -0.22, 0.18) if pieces else 1.0
    result = jax.random.normal(rng, dims, jnp.float32) * scale * factor_of
    return jnp.minimum(jnp.maximum(result, -reach), reach).astype(kind)


def setup_inputs(seed: int = 0, part: int = 0) -> dict:
    splits = jax.random.split(jax.random.key(seed), 9)
    own_keys = jax.random.split(jax.random.fold_in(splits[8], part), 9)
    return {
        "tokens": centred(own_keys[0], (TOK, D), 1.0, 6.0, ((1, 16),)),
        "token_scale": jnp.clip(jnp.exp(math.log(4.0) - 2.7725887 * jax.random.uniform(own_keys[1], (TOK, D // BLK), jnp.float32) ** steps_of(own_keys[1], (TOK, D // BLK), ((1, 16),), -0.2, 0.2)), 0.25, 4.0),
        "gate_tiles": centred(splits[2], (N_GX, D // RI, FF_SH // RO), D ** -0.5, 0.046875, ((0, 16),)),
        "up_tiles": centred(splits[3], (N_GX, D // RI, FF_SH // RO), D ** -0.5, 0.046875, ((0, 16),)),
        "gate_scale": jnp.clip(jnp.exp(jax.random.uniform(splits[4], (D // BLK, FF_SH // BLK), jnp.float32, math.log(0.25), math.log(4.0))), 0.25, 4.0),
        "up_scale": jnp.clip(jnp.exp(jax.random.uniform(splits[5], (D // BLK, FF_SH // BLK), jnp.float32, math.log(0.25), math.log(4.0))), 0.25, 4.0),
        "down_tiles": centred(splits[6], (N_GX, FF_SH // RO, D // RI), FF_SH ** -0.5, 0.078125, ((0, 16),)),
        "down_scale": jnp.clip(jnp.exp(jax.random.uniform(splits[7], (FF_SH // BLK, D // BLK), jnp.float32, math.log(0.25), math.log(4.0))), 0.25, 4.0),
    }


def scaled_matrix(stored, blocks):
    height, width = stored.shape
    expanded = stored.astype(jnp.float32).reshape(height // BLK, BLK, width // BLK, BLK)
    expanded = expanded * blocks[:, None, :, None]
    return expanded.reshape(height, width).astype(jnp.bfloat16)


def reference(tokens, token_scale, gate_tiles, up_tiles, gate_scale, up_scale, down_tiles, down_scale):
    count = tokens.shape[0]
    tile_rows = D // RI
    tile_cols = FF_SH // RO
    gate_weight = gate_tiles.reshape(RI, RO, tile_rows, tile_cols).transpose(0, 2, 1, 3).reshape(D, FF_SH)
    up_weight = up_tiles.reshape(RI, RO, tile_rows, tile_cols).transpose(0, 2, 1, 3).reshape(D, FF_SH)
    down_weight = down_tiles.reshape(RI, RO, tile_cols, tile_rows).transpose(1, 2, 0, 3).reshape(FF_SH, D)
    tokens_eff = tokens.astype(jnp.float32).reshape(count, D // BLK, BLK) * token_scale[:, :, None]
    tokens_eff = tokens_eff.reshape(count, D).astype(jnp.bfloat16)
    gate_eff = scaled_matrix(gate_weight, gate_scale)
    up_eff = scaled_matrix(up_weight, up_scale)
    down_eff = scaled_matrix(down_weight, down_scale)
    gate = jnp.dot(tokens_eff, gate_eff, preferred_element_type=jnp.float32)
    up_val = jnp.dot(tokens_eff, up_eff, preferred_element_type=jnp.float32)
    hidden = (jax.nn.silu(gate) * up_val).astype(jnp.bfloat16)
    return jnp.dot(hidden, down_eff, preferred_element_type=jnp.float32).astype(jnp.bfloat16)
```

```python
import jax
import jax.numpy as jnp
from jax import lax
from jax.sharding import PartitionSpec as P

BLK = 128
RO = 8
CHUNKS = 2


def partner(shard, mask):
    return lax.ppermute(shard, "gx", [(i, i ^ mask) for i in range(lax.axis_size("gx"))])


def from_behind(shard, by):
    devices = lax.axis_size("gx")
    return lax.ppermute(shard, "gx", [(i, (i + by) % devices) for i in range(devices)])


def scale_by_columns(stored, blocks, row_start, col_start):
    height, width = stored.shape
    row_scales = lax.dynamic_slice_in_dim(blocks, row_start // BLK, height // BLK, 0)
    owner = (col_start + jnp.arange(width, dtype=jnp.int32)) // BLK
    select = (jnp.arange(blocks.shape[1], dtype=jnp.int32)[:, None] == owner[None, :]).astype(
        jnp.float32
    )
    factors = jnp.dot(row_scales, select, precision=lax.Precision.HIGHEST)
    scaled = stored.astype(jnp.float32).reshape(height // BLK, BLK, width) * factors[:, None, :]
    return scaled.reshape(height, width).astype(jnp.bfloat16)


def scale_by_rows(stored, blocks, row_start, col_start):
    height, width = stored.shape
    col_scales = lax.dynamic_slice_in_dim(blocks, col_start // BLK, width // BLK, 1)
    owner = (row_start + jnp.arange(height, dtype=jnp.int32)) // BLK
    select = (owner[:, None] == jnp.arange(blocks.shape[0], dtype=jnp.int32)[None, :]).astype(
        jnp.float32
    )
    factors = jnp.dot(select, col_scales, precision=lax.Precision.HIGHEST)
    scaled = stored.astype(jnp.float32).reshape(height, width // BLK, BLK) * factors[:, :, None]
    return scaled.reshape(height, width).astype(jnp.bfloat16)


def gather_features(own, col_slot):
    width = own.shape[1]
    half = width // 2
    far = partner(own, 4)
    near = partner(own, 2)
    diagonal_a = partner(far[:, :half], 2)
    diagonal_b = partner(near[:, half:], 4)
    same = [
        (0, 0, own),
        (4, 0, far),
        (2, 0, near),
        (6, 0, diagonal_a),
        (6, half, diagonal_b),
    ]
    gathered = jnp.zeros((own.shape[0], width * RO), own.dtype)
    for mask, offset, block in same:
        gathered = lax.dynamic_update_slice_in_dim(
            gathered, block, (col_slot ^ mask) * width + offset, 1
        )
        gathered = lax.dynamic_update_slice_in_dim(
            gathered, partner(block, 1), (col_slot ^ mask ^ 1) * width + offset, 1
        )
    return gathered


def scatter_sum(result, col_slot):
    width = result.shape[1] // RO
    half = width // 2

    def piece(mask, offset, size):
        return lax.dynamic_slice_in_dim(result, (col_slot ^ mask) * width + offset, size, 1)

    def summed(mask, offset, size):
        sent = piece(mask ^ 1, offset, size).astype(jnp.bfloat16)
        return piece(mask, offset, size) + partner(sent, 1).astype(jnp.float32)

    def send(value, mask):
        return partner(value.astype(jnp.bfloat16), mask).astype(jnp.float32)

    diagonal_a = send(summed(6, 0, half), 2)
    diagonal_b = send(summed(6, half, half), 4)
    far_a = send(summed(4, 0, half) + diagonal_a, 4)
    far_b = send(summed(4, half, half), 4)
    near_a = send(summed(2, 0, half), 2)
    near_b = send(summed(2, half, half) + diagonal_b, 2)
    own_a = summed(0, 0, half) + far_a + near_a
    own_b = summed(0, half, half) + far_b + near_b
    return jnp.concatenate((own_a, own_b), 1).astype(jnp.bfloat16)


def body(tokens, token_scale, gate_tiles, up_tiles, gate_scale, up_scale, down_tiles, down_scale):
    position = lax.axis_index("gx")
    devices = lax.axis_size("gx")
    row_groups = devices // RO
    col_slot = position % RO
    row_slot = position // RO
    token_count, slice_width = tokens.shape
    tile_rows = gate_tiles.shape[1]
    tile_cols = gate_tiles.shape[2]
    piece_cols = tile_cols // row_groups
    tokens_eff = (
        tokens.astype(jnp.float32).reshape(token_count, slice_width // BLK, BLK)
        * token_scale[:, :, None]
    )
    tokens_eff = tokens_eff.reshape(token_count, slice_width).astype(jnp.bfloat16)
    gate_eff = scale_by_columns(
        gate_tiles[0], gate_scale, row_slot * tile_rows, col_slot * tile_cols
    )
    up_eff = scale_by_columns(up_tiles[0], up_scale, row_slot * tile_rows, col_slot * tile_cols)
    joined = jnp.concatenate((gate_eff, up_eff), 1)
    down_eff = scale_by_rows(down_tiles[0], down_scale, col_slot * tile_cols, row_slot * tile_rows)
    rows = token_count // CHUNKS

    def finish(gathered):
        partial_value = jnp.dot(gathered, joined, preferred_element_type=jnp.float32)

        def share(target):
            start = target * piece_cols
            return jnp.stack(
                (
                    lax.dynamic_slice_in_dim(partial_value, start, piece_cols, 1),
                    lax.dynamic_slice_in_dim(partial_value, tile_cols + start, piece_cols, 1),
                ),
                0,
            )

        summed = share((row_slot - 1) % row_groups)
        for step in range(1, row_groups):
            summed = from_behind(summed.astype(jnp.bfloat16), RO).astype(jnp.float32)
            summed = summed + share((row_slot - 1 - step) % row_groups)
        hidden_piece = (jax.nn.silu(summed[0]) * summed[1]).astype(jnp.bfloat16)
        hidden_full = jnp.zeros((rows, tile_cols), jnp.bfloat16)
        hidden_full = lax.dynamic_update_slice_in_dim(
            hidden_full, hidden_piece, row_slot * piece_cols, 1
        )
        current_hidden = hidden_piece
        for step in range(1, row_groups):
            current_hidden = from_behind(current_hidden, RO)
            source = (row_slot - step) % row_groups
            hidden_full = lax.dynamic_update_slice_in_dim(
                hidden_full, current_hidden, source * piece_cols, 1
            )
        result = jnp.dot(hidden_full, down_eff, preferred_element_type=jnp.float32)
        return scatter_sum(result, col_slot)

    outs = []
    for chunk in range(CHUNKS):
        own = tokens_eff[chunk * rows : (chunk + 1) * rows]
        outs.append(finish(gather_features(own, col_slot)))
    return jnp.concatenate(outs, 0)


def solution(mesh):
    return jax.shard_map(
        body,
        mesh=mesh,
        in_specs=(
            P("groups", "gx"),
            P("groups", "gx"),
            P("gx", None, None),
            P("gx", None, None),
            P(),
            P(),
            P("gx", None, None),
            P(),
        ),
        out_specs=P("groups", "gx"),
        check_vma=False,
    )
```

```python
import functools
import math

import jax
import jax.numpy as jnp
from jax import lax
from jax.experimental import pallas as pl
from jax.experimental.pallas import tpu as pltpu
from jax.sharding import PartitionSpec as P

BLK = 128
RO = 8
CHUNKS = 2
VMEM_BYTES = 56 * 2**20
GATHER_MASKS = (0, 1, 4, 5, 2, 3, 6, 7)
SENT_MASKS = (7, 5, 3, 1)
KEPT_MASKS = (6, 4, 2, 0)


def round_up(value, unit):
    return -(-value // unit) * unit


def partner(shard, mask):
    return lax.ppermute(shard, "gx", [(i, i ^ mask) for i in range(lax.axis_size("gx"))])


def from_behind(shard, by):
    devices = lax.axis_size("gx")
    return lax.ppermute(shard, "gx", [(i, (i + by) % devices) for i in range(devices)])


def params():
    return pltpu.CompilerParams(vmem_limit_bytes=VMEM_BYTES)


def cost(flops, moved):
    return pl.CostEstimate(flops=int(flops), bytes_accessed=int(moved), transcendentals=0)


def scale_tokens(tokens, token_scale):
    count, width = tokens.shape
    rows = count // CHUNKS

    def kernel(x_ref, s_ref, *out_refs):
        for chunk, out_ref in enumerate(out_refs):
            span = pl.ds(chunk * rows, rows)
            for block in range(width // BLK):
                columns = pl.ds(block * BLK, BLK)
                value = x_ref[span, columns].astype(jnp.float32)
                factor = s_ref[span, block : block + 1]
                out_ref[:, columns] = (value * factor).astype(jnp.bfloat16)

    return pl.pallas_call(
        kernel,
        out_shape=[jax.ShapeDtypeStruct((rows, width), jnp.bfloat16)] * CHUNKS,
        compiler_params=params(),
        cost_estimate=cost(count * width, 4 * count * width),
    )(tokens, token_scale)


def scale_joined(gate, up, gate_factors, up_factors):
    height, width = gate.shape
    padded = round_up(width, BLK)
    rows = min(1024, height)
    groups = rows // BLK

    def kernel(gate_ref, up_ref, gf_ref, uf_ref, out_ref):
        for index, (w_ref, f_ref) in enumerate(((gate_ref, gf_ref), (up_ref, uf_ref))):
            for group in range(groups):
                span = pl.ds(group * BLK, BLK)
                value = w_ref[span, :].astype(jnp.float32) * f_ref[group : group + 1, :]
                out_ref[span, index * padded : index * padded + width] = value.astype(jnp.bfloat16)
            if padded > width:
                out_ref[:, index * padded + width : (index + 1) * padded] = jnp.zeros(
                    (rows, padded - width), jnp.bfloat16
                )

    return pl.pallas_call(
        kernel,
        grid=(height // rows,),
        in_specs=[pl.BlockSpec((rows, width), lambda i: (i, 0))] * 2
        + [pl.BlockSpec((groups, width), lambda i: (i, 0))] * 2,
        out_specs=pl.BlockSpec((rows, 2 * padded), lambda i: (i, 0)),
        out_shape=jax.ShapeDtypeStruct((height, 2 * padded), jnp.bfloat16),
        compiler_params=params(),
        cost_estimate=cost(2 * height * width, 8 * height * width),
    )(gate, up, gate_factors, up_factors)


def scale_down(down, factors, unit):
    height, width = down.shape
    columns = min(1024, width)

    def kernel(w_ref, f_ref, out_ref):
        for group in range(height // unit):
            span = pl.ds(group * unit, unit)
            value = w_ref[span, :].astype(jnp.float32) * f_ref[group : group + 1, :]
            out_ref[span, :] = value.astype(jnp.bfloat16)

    return pl.pallas_call(
        kernel,
        grid=(width // columns,),
        in_specs=[
            pl.BlockSpec((height, columns), lambda i: (0, i)),
            pl.BlockSpec((factors.shape[0], columns), lambda i: (0, i)),
        ],
        out_specs=pl.BlockSpec((height, columns), lambda i: (0, i)),
        out_shape=jax.ShapeDtypeStruct((height, width), jnp.bfloat16),
        compiler_params=params(),
        cost_estimate=cost(height * width, 4 * height * width),
    )(down, factors)


def joined_product(slot, blocks, joined):
    width = blocks[0].shape[1]
    rows = blocks[0].shape[0]
    columns = joined.shape[1]
    flat = []
    places = []
    for block in blocks:
        parts = block if isinstance(block, tuple) else (block,)
        places.append(tuple(range(len(flat), len(flat) + len(parts))))
        flat.extend(parts)

    def mask_of(step):
        mask = step * 0
        for index, value in enumerate(GATHER_MASKS):
            mask = jnp.where(step == index, value, mask)
        return mask

    def kernel(slot_ref, *refs):
        x_refs, w_ref, out_ref = refs[: len(flat)], refs[len(flat)], refs[len(flat) + 1]
        step = pl.program_id(0)
        for index, place in enumerate(places):

            @pl.when(step == index)
            def _():
                parts = [x_refs[p][...] for p in place]
                x = parts[0] if len(parts) == 1 else jnp.concatenate(parts, 0)
                value = jnp.dot(x, w_ref[...], preferred_element_type=jnp.float32)
                if index == 0:
                    out_ref[...] = value
                else:
                    out_ref[...] += value

    return pl.pallas_call(
        kernel,
        grid_spec=pltpu.PrefetchScalarGridSpec(
            num_scalar_prefetch=1,
            grid=(len(places),),
            in_specs=[pl.BlockSpec(b.shape, lambda i, s: (0, 0)) for b in flat]
            + [pl.BlockSpec((width, columns), lambda i, s: (s[0] ^ mask_of(i), 0))],
            out_specs=pl.BlockSpec((rows, columns), lambda i, s: (0, 0)),
        ),
        out_shape=jax.ShapeDtypeStruct((rows, columns), jnp.float32),
        compiler_params=params(),
        cost_estimate=cost(2 * rows * width * RO * columns, 2 * width * RO * columns),
    )(slot, *flat, joined)


def output_product(slot, hidden, down, masks, kind):
    rows, depth = hidden.shape
    width = down.shape[1] // RO

    def mask_of(step):
        return masks[0] - 2 * step

    def kernel(slot_ref, x_ref, w_ref, out_ref):
        out_ref[0] = jnp.dot(
            x_ref[...], w_ref[...], preferred_element_type=jnp.float32
        ).astype(kind)

    return pl.pallas_call(
        kernel,
        grid_spec=pltpu.PrefetchScalarGridSpec(
            num_scalar_prefetch=1,
            grid=(len(masks),),
            in_specs=[
                pl.BlockSpec((rows, depth), lambda i, s: (0, 0)),
                pl.BlockSpec((depth, width), lambda i, s: (0, s[0] ^ mask_of(i))),
            ],
            out_specs=pl.BlockSpec((1, rows, width), lambda i, s: (i, 0, 0)),
        ),
        out_shape=jax.ShapeDtypeStruct((len(masks), rows, width), kind),
        compiler_params=params(),
        cost_estimate=cost(
            2 * rows * depth * len(masks) * width, 2 * depth * len(masks) * width
        ),
    )(slot, hidden, down)


def gather_features(own):
    half = own.shape[0] // 2
    far = partner(own, 4)
    near = partner(own, 2)
    upper = partner(far[:half], 2)
    lower = partner(near[half:], 4)
    return [
        own,
        partner(own, 1),
        far,
        partner(far, 1),
        near,
        partner(near, 1),
        (upper, lower),
        (partner(upper, 1), partner(lower, 1)),
    ]


def scatter_sum(sent, kept):
    half = sent.shape[1] // 2

    def summed(index, part):
        span = slice(part * half, (part + 1) * half)
        return kept[index, span] + partner(sent[index, span], 1).astype(jnp.float32)

    def send(value, mask):
        return partner(value.astype(jnp.bfloat16), mask).astype(jnp.float32)

    diagonal_a = send(summed(0, 0), 2)
    diagonal_b = send(summed(0, 1), 4)
    far_b = send(summed(1, 1), 4)
    near_a = send(summed(2, 0), 2)
    far_a = send(summed(1, 0) + diagonal_a, 4)
    near_b = send(summed(2, 1) + diagonal_b, 2)
    return [
        (summed(3, 0) + far_a + near_a).astype(jnp.bfloat16),
        (summed(3, 1) + far_b + near_b).astype(jnp.bfloat16),
    ]


def body(tokens, token_scale, gate_tiles, up_tiles, gate_scale, up_scale, down_tiles, down_scale):
    position = lax.axis_index("gx")
    devices = lax.axis_size("gx")
    row_groups = devices // RO
    col_slot = position % RO
    row_slot = position // RO
    slot = col_slot.astype(jnp.int32).reshape(1)
    token_count = tokens.shape[0]
    tile_rows = gate_tiles.shape[1]
    tile_cols = gate_tiles.shape[2]
    piece_cols = tile_cols // row_groups
    padded = round_up(tile_cols, BLK)
    unit = math.gcd(tile_cols, BLK)
    units = tile_cols // unit

    def column_factors(blocks):
        rows = lax.dynamic_slice_in_dim(
            blocks, row_slot * (tile_rows // BLK), tile_rows // BLK, 0
        )
        fine = jnp.repeat(rows, BLK // unit, 1)
        fine = lax.dynamic_slice_in_dim(fine, col_slot * units, units, 1)
        return jnp.repeat(fine, unit, 1)

    def row_factors(blocks):
        columns = lax.dynamic_slice_in_dim(
            blocks, row_slot * (tile_rows // BLK), tile_rows // BLK, 1
        )
        fine = jnp.repeat(columns, BLK // unit, 0)
        fine = lax.dynamic_slice_in_dim(fine, col_slot * units, units, 0)
        return jnp.repeat(fine, BLK, 1)

    tokens_eff = scale_tokens(tokens, token_scale)
    joined = scale_joined(
        gate_tiles[0], up_tiles[0], column_factors(gate_scale), column_factors(up_scale)
    )
    down_eff = scale_down(down_tiles[0], row_factors(down_scale), unit)
    rows = token_count // CHUNKS

    def finish(own):
        partial_value = joined_product(slot, gather_features(own), joined)

        def share(target):
            start = target * piece_cols
            return jnp.stack(
                (
                    lax.dynamic_slice_in_dim(partial_value, start, piece_cols, 1),
                    lax.dynamic_slice_in_dim(partial_value, padded + start, piece_cols, 1),
                ),
                0,
            )

        summed = share((row_slot - 1) % row_groups)
        for step in range(1, row_groups):
            summed = from_behind(summed.astype(jnp.bfloat16), RO).astype(jnp.float32)
            summed = summed + share((row_slot - 1 - step) % row_groups)
        hidden_piece = (jax.nn.silu(summed[0]) * summed[1]).astype(jnp.bfloat16)
        if row_groups == 2:
            other = from_behind(hidden_piece, RO)
            hidden_full = jnp.where(
                row_slot == 0,
                jnp.concatenate((hidden_piece, other), 1),
                jnp.concatenate((other, hidden_piece), 1),
            )
        else:
            hidden_full = jnp.zeros((rows, tile_cols), jnp.bfloat16)
            current = hidden_piece
            for step in range(row_groups):
                if step:
                    current = from_behind(current, RO)
                source = (row_slot - step) % row_groups
                hidden_full = lax.dynamic_update_slice_in_dim(
                    hidden_full, current, source * piece_cols, 1
                )
        sent = output_product(slot, hidden_full, down_eff, SENT_MASKS, jnp.bfloat16)
        kept = output_product(slot, hidden_full, down_eff, KEPT_MASKS, jnp.float32)
        return scatter_sum(sent, kept)

    outs = []
    for own in tokens_eff:
        outs.extend(finish(own))
    return jnp.concatenate(outs, 0)


def solution(mesh):
    return jax.shard_map(
        body,
        mesh=mesh,
        in_specs=(
            P("groups", "gx"),
            P("groups", "gx"),
            P("gx", None, None),
            P("gx", None, None),
            P(),
            P(),
            P("gx", None, None),
            P(),
        ),
        out_specs=P("groups", "gx"),
        check_vma=False,
    )
```

```python
import math

import jax
import jax.numpy as jnp
from jax import lax
from jax.experimental import pallas as pl
from jax.experimental.pallas import tpu as pltpu
from jax.sharding import PartitionSpec as P

BLK = 128
RO = 8
CHUNKS = 2
VMEM_BYTES = 56 * 2**20
GATHER_MASKS = (0, 1, 4, 5, 2, 3, 6, 7)
SENT_MASKS = (7, 5, 3, 1)
KEPT_MASKS = (6, 4, 2, 0)


def partner(shard, mask):
    return lax.ppermute(shard, "gx", [(i, i ^ mask) for i in range(lax.axis_size("gx"))])


def from_behind(shard, by):
    devices = lax.axis_size("gx")
    return lax.ppermute(shard, "gx", [(i, (i + by) % devices) for i in range(devices)])


def params():
    return pltpu.CompilerParams(vmem_limit_bytes=VMEM_BYTES)


def cost(flops, moved):
    return pl.CostEstimate(flops=int(flops), bytes_accessed=int(moved), transcendentals=0)


def scale_tokens(tokens, token_scale):
    count, width = tokens.shape
    rows = count // CHUNKS

    def kernel(x_ref, s_ref, *out_refs):
        factors = s_ref[...].T
        for chunk, out_ref in enumerate(out_refs):
            span = slice(chunk * rows, (chunk + 1) * rows)
            for block in range(width // BLK):
                columns = pl.ds(block * BLK, BLK)
                value = x_ref[span, columns].astype(jnp.float32)
                out_ref[:, columns] = (value * factors[span, block : block + 1]).astype(
                    jnp.bfloat16
                )

    return pl.pallas_call(
        kernel,
        out_shape=[jax.ShapeDtypeStruct((rows, width), jnp.bfloat16)] * CHUNKS,
        compiler_params=params(),
        cost_estimate=cost(count * width, 4 * count * width),
    )(tokens, token_scale.T)


def scale_rows(weights, factors, unit):
    height, width = weights[0].shape
    columns = width // RO
    many = len(weights)

    def kernel(*refs):
        out_ref = refs[-1]
        for index in range(many):
            w_ref, f_ref = refs[index], refs[many + index]
            for group in range(height // unit):
                span = pl.ds(group * unit, unit)
                value = w_ref[span, :].astype(jnp.float32) * f_ref[group : group + 1, :]
                out_ref[0, pl.ds(index * height + group * unit, unit), :] = value.astype(
                    jnp.bfloat16
                )

    return pl.pallas_call(
        kernel,
        grid=(RO,),
        in_specs=[pl.BlockSpec((height, columns), lambda i: (0, i))] * many
        + [pl.BlockSpec((height // unit, columns), lambda i: (0, i))] * many,
        out_specs=pl.BlockSpec((1, many * height, columns), lambda i: (i, 0, 0)),
        out_shape=jax.ShapeDtypeStruct((RO, many * height, columns), jnp.bfloat16),
        compiler_params=params(),
        cost_estimate=cost(many * height * width, 4 * many * height * width),
    )(*weights, *factors)


def joined_product(slot, blocks, joined):
    width = blocks[0].shape[1]
    rows = blocks[0].shape[0]
    height = joined.shape[1]
    flat = []
    places = []
    for block in blocks:
        parts = block if isinstance(block, tuple) else (block,)
        places.append(tuple(range(len(flat), len(flat) + len(parts))))
        flat.extend(parts)

    def mask_of(step):
        mask = step * 0
        for index, value in enumerate(GATHER_MASKS):
            mask = jnp.where(step == index, value, mask)
        return mask

    def kernel(slot_ref, *refs):
        x_refs, w_ref, out_ref = refs[: len(flat)], refs[len(flat)], refs[len(flat) + 1]
        step = pl.program_id(0)
        for index, place in enumerate(places):

            @pl.when(step == index)
            def _():
                parts = [x_refs[p][...] for p in place]
                x = parts[0] if len(parts) == 1 else jnp.concatenate(parts, 0)
                value = lax.dot_general(
                    w_ref[0], x, (((1,), (1,)), ((), ())), preferred_element_type=jnp.float32
                )
                if index == 0:
                    out_ref[...] = value
                else:
                    out_ref[...] += value

    return pl.pallas_call(
        kernel,
        grid_spec=pltpu.PrefetchScalarGridSpec(
            num_scalar_prefetch=1,
            grid=(len(places),),
            in_specs=[pl.BlockSpec(b.shape, lambda i, s: (0, 0)) for b in flat]
            + [pl.BlockSpec((1, height, width), lambda i, s: (s[0] ^ mask_of(i), 0, 0))],
            out_specs=pl.BlockSpec((height, rows), lambda i, s: (0, 0)),
        ),
        out_shape=jax.ShapeDtypeStruct((height, rows), jnp.float32),
        compiler_params=params(),
        cost_estimate=cost(2 * rows * width * RO * height, 2 * width * RO * height),
    )(slot, *flat, joined)


def output_product(slot, hidden, down, masks, kind):
    depth, rows = hidden.shape
    width = down.shape[2]

    def mask_of(step):
        return masks[0] - 2 * step

    def kernel(slot_ref, x_ref, w_ref, out_ref, turned):
        @pl.when(pl.program_id(0) == 0)
        def _():
            turned[...] = x_ref[...].T

        out_ref[0] = jnp.dot(
            turned[...], w_ref[0], preferred_element_type=jnp.float32
        ).astype(kind)

    return pl.pallas_call(
        kernel,
        grid_spec=pltpu.PrefetchScalarGridSpec(
            num_scalar_prefetch=1,
            grid=(len(masks),),
            in_specs=[
                pl.BlockSpec((depth, rows), lambda i, s: (0, 0)),
                pl.BlockSpec((1, depth, width), lambda i, s: (s[0] ^ mask_of(i), 0, 0)),
            ],
            out_specs=pl.BlockSpec((1, rows, width), lambda i, s: (i, 0, 0)),
            scratch_shapes=[pltpu.VMEM((rows, depth), jnp.bfloat16)],
        ),
        out_shape=jax.ShapeDtypeStruct((len(masks), rows, width), kind),
        compiler_params=params(),
        cost_estimate=cost(
            2 * rows * depth * len(masks) * width, 2 * depth * len(masks) * width
        ),
    )(slot, hidden, down)


def tie(*values):
    return lax.optimization_barrier(values)


def scatter_sum(sent, kept):
    half = sent.shape[1] // 2

    def summed(index, part):
        span = slice(part * half, (part + 1) * half)
        return kept[index, span] + partner(sent[index, span], 1).astype(jnp.float32)

    def send(value, mask):
        return partner(value.astype(jnp.bfloat16), mask).astype(jnp.float32)

    diagonal_a = send(summed(0, 0), 2)
    diagonal_b = send(summed(0, 1), 4)
    far_b = send(summed(1, 1), 4)
    near_a = send(summed(2, 0), 2)
    far_a = send(summed(1, 0) + diagonal_a, 4)
    near_b = send(summed(2, 1) + diagonal_b, 2)
    return [
        (summed(3, 0) + far_a + near_a).astype(jnp.bfloat16),
        (summed(3, 1) + far_b + near_b).astype(jnp.bfloat16),
    ]


def body(tokens, token_scale, gate_tiles, up_tiles, gate_scale, up_scale, down_tiles, down_scale):
    position = lax.axis_index("gx")
    devices = lax.axis_size("gx")
    row_groups = devices // RO
    col_slot = position % RO
    row_slot = position // RO
    slot = col_slot.astype(jnp.int32).reshape(1)
    token_count = tokens.shape[0]
    tile_rows = gate_tiles.shape[1]
    tile_cols = gate_tiles.shape[2]
    piece_cols = tile_cols // row_groups
    unit = math.gcd(tile_cols, BLK)
    units = tile_cols // unit

    first_block = row_slot * (tile_rows // BLK)

    def spread(blocks):
        columns = lax.dynamic_slice_in_dim(blocks, first_block, tile_rows // BLK, 1)
        fine = jnp.repeat(columns, BLK // unit, 0)
        fine = lax.dynamic_slice_in_dim(fine, col_slot * units, units, 0)
        return jnp.repeat(fine, BLK, 1)

    own_a, own_b = scale_tokens(tokens, token_scale)
    rows = token_count // CHUNKS
    half = rows // 2
    far_a, near_a = partner(own_a, 4), partner(own_a, 2)
    pair_a = partner(own_a, 1)
    far_b, near_b = partner(own_b, 4), partner(own_b, 2)
    pair_b = partner(own_b, 1)
    joined = scale_rows(
        (gate_tiles[0].T, up_tiles[0].T), (spread(gate_scale.T), spread(up_scale.T)), unit
    )
    far_a, near_a, pair_a, joined = tie(far_a, near_a, pair_a, joined)
    diagonal_a = partner(far_a[:half], 2), partner(near_a[half:], 4)
    far_pair_a, near_pair_a = partner(far_a, 1), partner(near_a, 1)
    down_eff = scale_rows((down_tiles[0],), (spread(down_scale),), unit)
    *diagonal_a, far_b, near_b, pair_b, down_eff = tie(
        *diagonal_a, far_b, near_b, pair_b, down_eff
    )

    def product(own, pair, far, far_pair, near, near_pair, diagonal):
        last = tuple(partner(part, 1) for part in diagonal)
        blocks = [own, pair, far, far_pair, near, near_pair, tuple(diagonal), last]
        return joined_product(slot, blocks, joined)

    def share(partial_value, target):
        start = target * piece_cols
        return jnp.stack(
            (
                lax.dynamic_slice_in_dim(partial_value, start, piece_cols, 0),
                lax.dynamic_slice_in_dim(partial_value, tile_cols + start, piece_cols, 0),
            ),
            0,
        )

    def first_share(partial_value):
        return share(partial_value, (row_slot - 1) % row_groups).astype(jnp.bfloat16)

    def hidden_of(sent, partial_value):
        summed = sent
        for step in range(1, row_groups):
            summed = from_behind(summed.astype(jnp.bfloat16), RO).astype(jnp.float32)
            summed = summed + share(partial_value, (row_slot - 1 - step) % row_groups)
        return (jax.nn.silu(summed[0]) * summed[1]).astype(jnp.bfloat16)

    def spread_hidden(piece):
        if row_groups == 2:
            other = from_behind(piece, RO)
            return jnp.where(
                row_slot == 0,
                jnp.concatenate((piece, other), 0),
                jnp.concatenate((other, piece), 0),
            )
        full = jnp.zeros((tile_cols, rows), jnp.bfloat16)
        current = piece
        for step in range(row_groups):
            if step:
                current = from_behind(current, RO)
            source = (row_slot - step) % row_groups
            full = lax.dynamic_update_slice_in_dim(full, current, source * piece_cols, 0)
        return full

    def output(hidden):
        sent = output_product(slot, hidden, down_eff, SENT_MASKS, jnp.bfloat16)
        kept = output_product(slot, hidden, down_eff, KEPT_MASKS, jnp.float32)
        return scatter_sum(sent, kept)

    partial_a = product(own_a, pair_a, far_a, far_pair_a, near_a, near_pair_a, diagonal_a)
    sent_a = first_share(partial_a)
    diagonal_b = partner(far_b[:half], 2), partner(near_b[half:], 4)
    far_pair_b, near_pair_b = partner(far_b, 1), partner(near_b, 1)
    *diagonal_b, partial_a = tie(*diagonal_b, partial_a)
    partial_b = product(own_b, pair_b, far_b, far_pair_b, near_b, near_pair_b, diagonal_b)
    piece_a = hidden_of(sent_a, partial_a)
    sent_b = first_share(partial_b)
    piece_a, sent_b = tie(piece_a, sent_b)
    piece_b = hidden_of(sent_b, partial_b)
    out_a = output(spread_hidden(piece_a))
    out_b = output(spread_hidden(piece_b))
    return jnp.concatenate(out_a + out_b, 0)


def solution(mesh):
    return jax.shard_map(
        body,
        mesh=mesh,
        in_specs=(
            P("groups", "gx"),
            P("groups", "gx"),
            P("gx", None, None),
            P("gx", None, None),
            P(),
            P(),
            P("gx", None, None),
            P(),
        ),
        out_specs=P("groups", "gx"),
        check_vma=False,
    )
```

```python
import math

import jax
import jax.numpy as jnp
from jax import lax
from jax.experimental import pallas as pl
from jax.experimental.pallas import tpu as pltpu
from jax.sharding import PartitionSpec as P

BLK = 128
RO = 8
CHUNKS = 2
VMEM_BYTES = 56 * 2**20
FIRST_MASKS = (0, 1, 4, 5, 2, 3)
LAST_MASKS = (6, 7)
SENT_MASKS = (7, 5, 3, 1)
KEPT_MASKS = (6, 4, 2, 0)


def partner(shard, mask):
    return lax.ppermute(shard, "gx", [(i, i ^ mask) for i in range(lax.axis_size("gx"))])


def from_behind(shard, by):
    devices = lax.axis_size("gx")
    return lax.ppermute(shard, "gx", [(i, (i + by) % devices) for i in range(devices)])


def params():
    return pltpu.CompilerParams(vmem_limit_bytes=VMEM_BYTES)


def cost(flops, moved):
    return pl.CostEstimate(flops=int(flops), bytes_accessed=int(moved), transcendentals=0)


def scale_tokens(tokens, token_scale):
    count, width = tokens.shape
    rows = count // CHUNKS

    def kernel(x_ref, s_ref, *out_refs):
        factors = s_ref[...].T
        for chunk, out_ref in enumerate(out_refs):
            span = slice(chunk * rows, (chunk + 1) * rows)
            for block in range(width // BLK):
                columns = pl.ds(block * BLK, BLK)
                value = x_ref[span, columns].astype(jnp.float32)
                out_ref[:, columns] = (value * factors[span, block : block + 1]).astype(
                    jnp.bfloat16
                )

    return pl.pallas_call(
        kernel,
        out_shape=[jax.ShapeDtypeStruct((rows, width), jnp.bfloat16)] * CHUNKS,
        compiler_params=params(),
        cost_estimate=cost(count * width, 4 * count * width),
    )(tokens, token_scale.T)


def scale_rows(weights, factors, unit):
    height, width = weights[0].shape
    columns = width // RO
    many = len(weights)

    def kernel(*refs):
        out_ref = refs[-1]
        for index in range(many):
            w_ref, f_ref = refs[index], refs[many + index]
            for group in range(height // unit):
                span = pl.ds(group * unit, unit)
                value = w_ref[span, :].astype(jnp.float32) * f_ref[group : group + 1, :]
                out_ref[0, pl.ds(index * height + group * unit, unit), :] = value.astype(
                    jnp.bfloat16
                )

    return pl.pallas_call(
        kernel,
        grid=(RO,),
        in_specs=[pl.BlockSpec((height, columns), lambda i: (0, i))] * many
        + [pl.BlockSpec((height // unit, columns), lambda i: (0, i))] * many,
        out_specs=pl.BlockSpec((1, many * height, columns), lambda i: (i, 0, 0)),
        out_shape=jax.ShapeDtypeStruct((RO, many * height, columns), jnp.bfloat16),
        compiler_params=params(),
        cost_estimate=cost(many * height * width, 4 * many * height * width),
    )(*weights, *factors)


def joined_product(slot, blocks, masks, joined, before=None):
    width = joined.shape[2]
    rows = sum(part.shape[0] for part in blocks[0]) if isinstance(blocks[0], tuple) else blocks[0].shape[0]
    height = joined.shape[1]
    flat = []
    places = []
    for block in blocks:
        parts = block if isinstance(block, tuple) else (block,)
        places.append(tuple(range(len(flat), len(flat) + len(parts))))
        flat.extend(parts)

    extra = () if before is None else (before,)

    def mask_of(step):
        mask = step * 0
        for index, value in enumerate(masks):
            mask = jnp.where(step == index, value, mask)
        return mask

    def kernel(slot_ref, *refs):
        x_refs, w_ref, out_ref = refs[: len(flat)], refs[len(flat)], refs[-1]
        step = pl.program_id(0)
        for index, place in enumerate(places):

            @pl.when(step == index)
            def _():
                parts = [x_refs[p][...] for p in place]
                x = parts[0] if len(parts) == 1 else jnp.concatenate(parts, 0)
                value = lax.dot_general(
                    w_ref[0], x, (((1,), (1,)), ((), ())), preferred_element_type=jnp.float32
                )
                if index == 0 and before is None:
                    out_ref[...] = value
                elif index == 0:
                    out_ref[...] = refs[-2][...] + value
                else:
                    out_ref[...] += value

    return pl.pallas_call(
        kernel,
        grid_spec=pltpu.PrefetchScalarGridSpec(
            num_scalar_prefetch=1,
            grid=(len(places),),
            in_specs=[pl.BlockSpec(b.shape, lambda i, s: (0, 0)) for b in flat]
            + [pl.BlockSpec((1, height, width), lambda i, s: (s[0] ^ mask_of(i), 0, 0))]
            + [pl.BlockSpec((height, rows), lambda i, s: (0, 0))] * len(extra),
            out_specs=pl.BlockSpec((height, rows), lambda i, s: (0, 0)),
        ),
        out_shape=jax.ShapeDtypeStruct((height, rows), jnp.float32),
        compiler_params=params(),
        cost_estimate=cost(
            2 * rows * width * len(masks) * height, 2 * width * len(masks) * height
        ),
    )(slot, *flat, joined, *extra)


def output_product(slot, hidden, down, masks, kind):
    depth, rows = hidden.shape
    width = down.shape[2]

    def mask_of(step):
        return masks[0] - 2 * step

    def kernel(slot_ref, x_ref, w_ref, out_ref, turned):
        @pl.when(pl.program_id(0) == 0)
        def _():
            turned[...] = x_ref[...].T

        out_ref[0] = jnp.dot(
            turned[...], w_ref[0], preferred_element_type=jnp.float32
        ).astype(kind)

    return pl.pallas_call(
        kernel,
        grid_spec=pltpu.PrefetchScalarGridSpec(
            num_scalar_prefetch=1,
            grid=(len(masks),),
            in_specs=[
                pl.BlockSpec((depth, rows), lambda i, s: (0, 0)),
                pl.BlockSpec((1, depth, width), lambda i, s: (s[0] ^ mask_of(i), 0, 0)),
            ],
            out_specs=pl.BlockSpec((1, rows, width), lambda i, s: (i, 0, 0)),
            scratch_shapes=[pltpu.VMEM((rows, depth), jnp.bfloat16)],
        ),
        out_shape=jax.ShapeDtypeStruct((len(masks), rows, width), kind),
        compiler_params=params(),
        cost_estimate=cost(
            2 * rows * depth * len(masks) * width, 2 * depth * len(masks) * width
        ),
    )(slot, hidden, down)


def tie(*values):
    return lax.optimization_barrier(values)


def exchange_pair(sent, kept):
    first = kept[0] + partner(sent[0], 1).astype(jnp.float32)
    rest = partner(sent[1:], 1)
    return first.astype(jnp.bfloat16), rest


def forward(diagonal, rest, kept, by_y):
    arrived = partner(diagonal, 2 if by_y else 4).astype(jnp.float32)
    far = kept[1] + rest[0].astype(jnp.float32)
    near = kept[2] + rest[1].astype(jnp.float32)
    if by_y:
        far = far + arrived
    else:
        near = near + arrived
    return far.astype(jnp.bfloat16), near.astype(jnp.bfloat16)


def collect(far, near, rest, kept):
    total = kept[3] + rest[2].astype(jnp.float32)
    total = total + partner(far, 4).astype(jnp.float32) + partner(near, 2).astype(jnp.float32)
    return total.astype(jnp.bfloat16)


def body(tokens, token_scale, gate_tiles, up_tiles, gate_scale, up_scale, down_tiles, down_scale):
    position = lax.axis_index("gx")
    devices = lax.axis_size("gx")
    row_groups = devices // RO
    col_slot = position % RO
    row_slot = position // RO
    slot = col_slot.astype(jnp.int32).reshape(1)
    token_count = tokens.shape[0]
    tile_rows = gate_tiles.shape[1]
    tile_cols = gate_tiles.shape[2]
    piece_cols = tile_cols // row_groups
    unit = math.gcd(tile_cols, BLK)
    units = tile_cols // unit

    first_block = row_slot * (tile_rows // BLK)

    def spread(blocks):
        columns = lax.dynamic_slice_in_dim(blocks, first_block, tile_rows // BLK, 1)
        fine = jnp.repeat(columns, BLK // unit, 0)
        fine = lax.dynamic_slice_in_dim(fine, col_slot * units, units, 0)
        return jnp.repeat(fine, BLK, 1)

    own_a, own_b = scale_tokens(tokens, token_scale)
    rows = token_count // CHUNKS
    half = rows // 2
    far_a, near_a = partner(own_a, 4), partner(own_a, 2)
    pair_a = partner(own_a, 1)
    far_b, near_b = partner(own_b, 4), partner(own_b, 2)
    joined = scale_rows(
        (gate_tiles[0].T, up_tiles[0].T), (spread(gate_scale.T), spread(up_scale.T)), unit
    )
    far_a, near_a, pair_a, own_b, joined = tie(far_a, near_a, pair_a, own_b, joined)
    diagonal_a = partner(far_a[:half], 2), partner(near_a[half:], 4)
    far_pair_a, near_pair_a = partner(far_a, 1), partner(near_a, 1)
    pair_b = partner(own_b, 1)

    def pairs(diagonal):
        return [tuple(diagonal), tuple(partner(part, 1) for part in diagonal)]

    def share(partial_value, target):
        start = target * piece_cols
        return jnp.stack(
            (
                lax.dynamic_slice_in_dim(partial_value, start, piece_cols, 0),
                lax.dynamic_slice_in_dim(partial_value, tile_cols + start, piece_cols, 0),
            ),
            0,
        )

    def first_share(partial_value):
        return share(partial_value, (row_slot - 1) % row_groups).astype(jnp.bfloat16)

    def hidden_of(sent, partial_value):
        summed = sent
        for step in range(1, row_groups):
            summed = from_behind(summed.astype(jnp.bfloat16), RO).astype(jnp.float32)
            summed = summed + share(partial_value, (row_slot - 1 - step) % row_groups)
        return (jax.nn.silu(summed[0]) * summed[1]).astype(jnp.bfloat16)

    def spread_hidden(piece):
        if row_groups == 2:
            other = from_behind(piece, RO)
            return jnp.where(
                row_slot == 0,
                jnp.concatenate((piece, other), 0),
                jnp.concatenate((other, piece), 0),
            )
        full = jnp.zeros((tile_cols, rows), jnp.bfloat16)
        current = piece
        for step in range(row_groups):
            if step:
                current = from_behind(current, RO)
            source = (row_slot - step) % row_groups
            full = lax.dynamic_update_slice_in_dim(full, current, source * piece_cols, 0)
        return full

    blocks_a = [own_a, pair_a, far_a, far_pair_a, near_a, near_pair_a]
    partial_a = joined_product(slot, blocks_a, FIRST_MASKS, joined)
    *diagonal_a, far_b, near_b, pair_b, partial_a = tie(
        *diagonal_a, far_b, near_b, pair_b, partial_a
    )
    last_a = pairs(diagonal_a)
    diagonal_b = partner(far_b[:half], 2), partner(near_b[half:], 4)
    far_pair_b, near_pair_b = partner(far_b, 1), partner(near_b, 1)
    partial_a = joined_product(slot, last_a, LAST_MASKS, joined, partial_a)
    sent_a = first_share(partial_a)
    *diagonal_b, far_pair_b, near_pair_b, sent_a = tie(
        *diagonal_b, far_pair_b, near_pair_b, sent_a
    )
    blocks_b = [own_b, pair_b, far_b, far_pair_b, near_b, near_pair_b] + pairs(diagonal_b)
    partial_b = joined_product(slot, blocks_b, FIRST_MASKS + LAST_MASKS, joined)
    piece_a = hidden_of(sent_a, partial_a)
    sent_b = first_share(partial_b)
    piece_a, sent_b, factors = tie(piece_a, sent_b, spread(down_scale))
    down_eff = scale_rows((down_tiles[0],), (factors,), unit)
    hidden_a = spread_hidden(piece_a)
    hidden_a, down_eff = tie(hidden_a, down_eff)
    piece_b = hidden_of(sent_b, partial_b)

    def sent_product(hidden):
        return output_product(slot, hidden, down_eff, SENT_MASKS, jnp.bfloat16)

    def kept_product(hidden):
        return output_product(slot, hidden, down_eff, KEPT_MASKS, jnp.float32)

    to_pair_a, kept_a = sent_product(hidden_a), kept_product(hidden_a)
    diagonal, rest_a = exchange_pair(to_pair_a, kept_a)
    hidden_b = spread_hidden(piece_b)
    diagonal, hidden_b = tie(diagonal, hidden_b)
    to_pair_b = sent_product(hidden_b)
    forward_a = forward(diagonal, rest_a, kept_a, True)
    *forward_a, hidden_b = tie(*forward_a, hidden_b)
    kept_b = kept_product(hidden_b)
    diagonal, rest_b = exchange_pair(to_pair_b, kept_b)
    forward_b = forward(diagonal, rest_b, kept_b, False)
    out_a = collect(*forward_a, rest_a, kept_a)
    out_b = collect(*forward_b, rest_b, kept_b)
    return jnp.concatenate((out_a, out_b), 0)


def solution(mesh):
    return jax.shard_map(
        body,
        mesh=mesh,
        in_specs=(
            P("groups", "gx"),
            P("groups", "gx"),
            P("gx", None, None),
            P("gx", None, None),
            P(),
            P(),
            P("gx", None, None),
            P(),
        ),
        out_specs=P("groups", "gx"),
        check_vma=False,
    )
```

```python
import math

import jax
import jax.numpy as jnp
from jax import lax
from jax.experimental import pallas as pl
from jax.experimental.pallas import tpu as pltpu
from jax.sharding import PartitionSpec as P

BLK = 128
RO = 8
CHUNKS = 2
VMEM_BYTES = 56 * 2**20
FIRST_MASKS = (0, 1, 4, 5, 2, 3)
LAST_MASKS = (6, 7)
SENT_MASKS = (7, 5, 3, 1)
KEPT_MASKS = (6, 4, 2, 0)


def partner(shard, mask):
    return lax.ppermute(shard, "gx", [(i, i ^ mask) for i in range(lax.axis_size("gx"))])


def from_behind(shard, by):
    devices = lax.axis_size("gx")
    return lax.ppermute(shard, "gx", [(i, (i + by) % devices) for i in range(devices)])


def params():
    return pltpu.CompilerParams(vmem_limit_bytes=VMEM_BYTES)


def cost(flops, moved):
    return pl.CostEstimate(flops=int(flops), bytes_accessed=int(moved), transcendentals=0)


def scale_tokens(tokens, token_scale):
    count, width = tokens.shape
    rows = count // CHUNKS

    def kernel(x_ref, s_ref, *out_refs):
        factors = s_ref[...].T
        for chunk, out_ref in enumerate(out_refs):
            span = slice(chunk * rows, (chunk + 1) * rows)
            for block in range(width // BLK):
                columns = pl.ds(block * BLK, BLK)
                value = x_ref[span, columns].astype(jnp.float32)
                out_ref[:, columns] = (value * factors[span, block : block + 1]).astype(
                    jnp.bfloat16
                )

    return pl.pallas_call(
        kernel,
        out_shape=[jax.ShapeDtypeStruct((rows, width), jnp.bfloat16)] * CHUNKS,
        compiler_params=params(),
        cost_estimate=cost(count * width, 4 * count * width),
    )(tokens, token_scale.T)


def scale_rows(weights, factors, unit):
    height, width = weights[0].shape
    columns = width // RO
    many = len(weights)

    def kernel(*refs):
        out_ref = refs[-1]
        for index in range(many):
            w_ref, f_ref = refs[index], refs[many + index]
            for group in range(height // unit):
                span = pl.ds(group * unit, unit)
                value = w_ref[span, :].astype(jnp.float32) * f_ref[group : group + 1, :]
                out_ref[0, pl.ds(index * height + group * unit, unit), :] = value.astype(
                    jnp.bfloat16
                )

    return pl.pallas_call(
        kernel,
        grid=(RO,),
        in_specs=[pl.BlockSpec((height, columns), lambda i: (0, i))] * many
        + [pl.BlockSpec((height // unit, columns), lambda i: (0, i))] * many,
        out_specs=pl.BlockSpec((1, many * height, columns), lambda i: (i, 0, 0)),
        out_shape=jax.ShapeDtypeStruct((RO, many * height, columns), jnp.bfloat16),
        compiler_params=params(),
        cost_estimate=cost(many * height * width, 4 * many * height * width),
    )(*weights, *factors)


def joined_product(slot, blocks, masks, joined, before=None):
    width = joined.shape[2]
    rows = sum(part.shape[0] for part in blocks[0]) if isinstance(blocks[0], tuple) else blocks[0].shape[0]
    height = joined.shape[1]
    flat = []
    places = []
    for block in blocks:
        parts = block if isinstance(block, tuple) else (block,)
        places.append(tuple(range(len(flat), len(flat) + len(parts))))
        flat.extend(parts)

    extra = () if before is None else (before,)

    def mask_of(step):
        mask = step * 0
        for index, value in enumerate(masks):
            mask = jnp.where(step == index, value, mask)
        return mask

    def kernel(slot_ref, *refs):
        x_refs, w_ref, out_ref = refs[: len(flat)], refs[len(flat)], refs[-1]
        step = pl.program_id(0)
        for index, place in enumerate(places):

            @pl.when(step == index)
            def _():
                parts = [x_refs[p][...] for p in place]
                x = parts[0] if len(parts) == 1 else jnp.concatenate(parts, 0)
                value = lax.dot_general(
                    w_ref[0], x, (((1,), (1,)), ((), ())), preferred_element_type=jnp.float32
                )
                if index == 0 and before is None:
                    out_ref[...] = value
                elif index == 0:
                    out_ref[...] = refs[-2][...] + value
                else:
                    out_ref[...] += value

    return pl.pallas_call(
        kernel,
        grid_spec=pltpu.PrefetchScalarGridSpec(
            num_scalar_prefetch=1,
            grid=(len(places),),
            in_specs=[pl.BlockSpec(b.shape, lambda i, s: (0, 0)) for b in flat]
            + [pl.BlockSpec((1, height, width), lambda i, s: (s[0] ^ mask_of(i), 0, 0))]
            + [pl.BlockSpec((height, rows), lambda i, s: (0, 0))] * len(extra),
            out_specs=pl.BlockSpec((height, rows), lambda i, s: (0, 0)),
        ),
        out_shape=jax.ShapeDtypeStruct((height, rows), jnp.float32),
        compiler_params=params(),
        cost_estimate=cost(
            2 * rows * width * len(masks) * height, 2 * width * len(masks) * height
        ),
    )(slot, *flat, joined, *extra)


def output_product(slot, hidden, down, masks, kind):
    depth, rows = hidden.shape
    width = down.shape[2]

    def mask_of(step):
        return masks[0] - 2 * step

    def kernel(slot_ref, x_ref, w_ref, out_ref, turned):
        @pl.when(pl.program_id(0) == 0)
        def _():
            turned[...] = x_ref[...].T

        out_ref[0] = jnp.dot(
            turned[...], w_ref[0], preferred_element_type=jnp.float32
        ).astype(kind)

    return pl.pallas_call(
        kernel,
        grid_spec=pltpu.PrefetchScalarGridSpec(
            num_scalar_prefetch=1,
            grid=(len(masks),),
            in_specs=[
                pl.BlockSpec((depth, rows), lambda i, s: (0, 0)),
                pl.BlockSpec((1, depth, width), lambda i, s: (s[0] ^ mask_of(i), 0, 0)),
            ],
            out_specs=pl.BlockSpec((1, rows, width), lambda i, s: (i, 0, 0)),
            scratch_shapes=[pltpu.VMEM((rows, depth), jnp.bfloat16)],
        ),
        out_shape=jax.ShapeDtypeStruct((len(masks), rows, width), kind),
        compiler_params=params(),
        cost_estimate=cost(
            2 * rows * depth * len(masks) * width, 2 * depth * len(masks) * width
        ),
    )(slot, hidden, down)


def tie(*values):
    return lax.optimization_barrier(values)


def exchange_pair(sent, kept):
    first = kept[0] + partner(sent[0], 1).astype(jnp.float32)
    rest = partner(sent[1:], 1)
    return first.astype(jnp.bfloat16), rest


def forward(diagonal, rest, kept, halves):
    far = kept[1] + rest[0].astype(jnp.float32)
    near = kept[2] + rest[1].astype(jnp.float32)
    if halves:
        half = diagonal.shape[0] // 2
        upper = partner(diagonal[:half], 2).astype(jnp.float32)
        lower = partner(diagonal[half:], 4).astype(jnp.float32)
        far = jnp.concatenate((far[:half] + upper, far[half:]), 0)
        near = jnp.concatenate((near[:half], near[half:] + lower), 0)
    else:
        far = far + partner(diagonal, 2).astype(jnp.float32)
    return far.astype(jnp.bfloat16), near.astype(jnp.bfloat16)


def collect(far, near, rest, kept):
    total = kept[3] + rest[2].astype(jnp.float32)
    total = total + partner(far, 4).astype(jnp.float32) + partner(near, 2).astype(jnp.float32)
    return total.astype(jnp.bfloat16)


def body(tokens, token_scale, gate_tiles, up_tiles, gate_scale, up_scale, down_tiles, down_scale):
    position = lax.axis_index("gx")
    devices = lax.axis_size("gx")
    row_groups = devices // RO
    col_slot = position % RO
    row_slot = position // RO
    slot = col_slot.astype(jnp.int32).reshape(1)
    token_count = tokens.shape[0]
    tile_rows = gate_tiles.shape[1]
    tile_cols = gate_tiles.shape[2]
    piece_cols = tile_cols // row_groups
    unit = math.gcd(tile_cols, BLK)
    units = tile_cols // unit

    first_block = row_slot * (tile_rows // BLK)

    def spread(blocks):
        columns = lax.dynamic_slice_in_dim(blocks, first_block, tile_rows // BLK, 1)
        fine = jnp.repeat(columns, BLK // unit, 0)
        fine = lax.dynamic_slice_in_dim(fine, col_slot * units, units, 0)
        return jnp.repeat(fine, BLK, 1)

    own_a, own_b = scale_tokens(tokens, token_scale)
    rows = token_count // CHUNKS
    half = rows // 2
    far_a, near_a = partner(own_a, 4), partner(own_a, 2)
    pair_a = partner(own_a, 1)
    far_b, near_b = partner(own_b, 4), partner(own_b, 2)
    joined = scale_rows(
        (gate_tiles[0].T, up_tiles[0].T), (spread(gate_scale.T), spread(up_scale.T)), unit
    )
    far_a, near_a, pair_a, own_b, joined = tie(far_a, near_a, pair_a, own_b, joined)
    diagonal_a = partner(far_a[:half], 2), partner(near_a[half:], 4)
    far_pair_a, near_pair_a = partner(far_a, 1), partner(near_a, 1)
    pair_b = partner(own_b, 1)

    def pairs(diagonal):
        return [tuple(diagonal), tuple(partner(part, 1) for part in diagonal)]

    def share(partial_value, target):
        start = target * piece_cols
        return jnp.stack(
            (
                lax.dynamic_slice_in_dim(partial_value, start, piece_cols, 0),
                lax.dynamic_slice_in_dim(partial_value, tile_cols + start, piece_cols, 0),
            ),
            0,
        )

    def first_share(partial_value):
        return share(partial_value, (row_slot - 1) % row_groups).astype(jnp.bfloat16)

    def hidden_of(sent, partial_value):
        summed = sent
        for step in range(1, row_groups):
            summed = from_behind(summed.astype(jnp.bfloat16), RO).astype(jnp.float32)
            summed = summed + share(partial_value, (row_slot - 1 - step) % row_groups)
        return (jax.nn.silu(summed[0]) * summed[1]).astype(jnp.bfloat16)

    def spread_hidden(piece):
        if row_groups == 2:
            other = from_behind(piece, RO)
            return jnp.where(
                row_slot == 0,
                jnp.concatenate((piece, other), 0),
                jnp.concatenate((other, piece), 0),
            )
        full = jnp.zeros((tile_cols, rows), jnp.bfloat16)
        current = piece
        for step in range(row_groups):
            if step:
                current = from_behind(current, RO)
            source = (row_slot - step) % row_groups
            full = lax.dynamic_update_slice_in_dim(full, current, source * piece_cols, 0)
        return full

    blocks_a = [own_a, pair_a, far_a, far_pair_a, near_a, near_pair_a]
    partial_a = joined_product(slot, blocks_a, FIRST_MASKS, joined)
    *diagonal_a, far_b, near_b, pair_b, partial_a = tie(
        *diagonal_a, far_b, near_b, pair_b, partial_a
    )
    last_a = pairs(diagonal_a)
    diagonal_b = partner(far_b[:half], 2), partner(near_b[half:], 4)
    far_pair_b, near_pair_b = partner(far_b, 1), partner(near_b, 1)
    partial_a = joined_product(slot, last_a, LAST_MASKS, joined, partial_a)
    sent_a = first_share(partial_a)
    *diagonal_b, far_pair_b, near_pair_b, sent_a = tie(
        *diagonal_b, far_pair_b, near_pair_b, sent_a
    )
    blocks_b = [own_b, pair_b, far_b, far_pair_b, near_b, near_pair_b] + pairs(diagonal_b)
    partial_b = joined_product(slot, blocks_b, FIRST_MASKS + LAST_MASKS, joined)
    piece_a = hidden_of(sent_a, partial_a)
    sent_b = first_share(partial_b)
    piece_a, sent_b, factors = tie(piece_a, sent_b, spread(down_scale))
    down_eff = scale_rows((down_tiles[0],), (factors,), unit)
    hidden_a = spread_hidden(piece_a)
    hidden_a, down_eff = tie(hidden_a, down_eff)
    piece_b = hidden_of(sent_b, partial_b)

    def sent_product(hidden):
        return output_product(slot, hidden, down_eff, SENT_MASKS, jnp.bfloat16)

    def kept_product(hidden):
        return output_product(slot, hidden, down_eff, KEPT_MASKS, jnp.float32)

    to_pair_a, kept_a = sent_product(hidden_a), kept_product(hidden_a)
    diagonal, rest_a = exchange_pair(to_pair_a, kept_a)
    hidden_b = spread_hidden(piece_b)
    diagonal, hidden_b = tie(diagonal, hidden_b)
    to_pair_b = sent_product(hidden_b)
    forward_a = forward(diagonal, rest_a, kept_a, False)
    *forward_a, hidden_b = tie(*forward_a, hidden_b)
    kept_b = kept_product(hidden_b)
    diagonal, rest_b = exchange_pair(to_pair_b, kept_b)
    forward_b = forward(diagonal, rest_b, kept_b, True)
    out_a = collect(*forward_a, rest_a, kept_a)
    out_b = collect(*forward_b, rest_b, kept_b)
    return jnp.concatenate((out_a, out_b), 0)


def solution(mesh):
    return jax.shard_map(
        body,
        mesh=mesh,
        in_specs=(
            P("groups", "gx"),
            P("groups", "gx"),
            P("gx", None, None),
            P("gx", None, None),
            P(),
            P(),
            P("gx", None, None),
            P(),
        ),
        out_specs=P("groups", "gx"),
        check_vma=False,
    )
```
